32 devices in a mesh: users: 8 (over z, x), items: 4 (over y, core).
Axes of the slice: x: 2, y: 2, z: 4, core: 2. Of those that a mesh axis runs over, the one named last changes fastest.
Arguments:
- interactions: bfloat16 [16384, 32768], P('users', 'items'), may hold values from 0 to 13, as said below
- user_weights: bfloat16 [16384], P('users'), may hold values from 0.3 to 9, as said below
- panel_index: int32 [1], replicated, may hold values from 0 to 127
Outputs:
- item_covariance: float32 [32, 1024, 256], P(None, ('users', 'items'))
- item_mean: float32 [32, 1024], P(None, ('users', 'items'))
The draws below stay inside these ranges and needn't reach their ends.
Inputs may be any that keep to these rules, and one draw needn't show every extreme that they name: `user_weights`: positive user weights. `interactions`: confidences are zero or positive.
All inputs are finite; a program needn't handle non-finite values.
Results may differ from the reference program's by a relative error of at most 0.00031.
Values may be sent and summed in bfloat16 or wider, within the bound.
A program may use at most 384 MiB of HBM per device.

```python
import jax
import jax.numpy as jnp
from jax import lax

N = 32768
P_SIZE = 256
BLK = 32
USR_DEV = 2048
USERS = 16384
CYC = 32
N_USERS = 8
N_ITEMS = 4


def draw_interactions(key, part):
    key = jax.random.fold_in(key, 11)
    keys = jax.random.split(key, 4)
    activity = jnp.clip(0.7 * jax.random.normal(keys[0], (USERS, 1), jnp.float32), -2.1, 2.1)
    spread = jax.random.uniform(keys[1], (USERS, N), jnp.float32, 0.5, 1.5)
    popular = jax.random.uniform(keys[2], (1, N), jnp.float32, 0.3, 0.8)
    chance = jax.random.uniform(keys[3], (USERS, N), jnp.float32)
    present = jnp.where(chance < popular, 1.0, 0.0)
    return (present * jnp.exp(activity) * spread).astype(jnp.bfloat16)


def draw_user_weights(key, part):
    key = jax.random.fold_in(key, 23)
    base = jnp.exp(jax.random.uniform(key, (USERS,), jnp.float32, jnp.log(0.3), jnp.log(3.0)))
    ramp = 1.0 + 2.0 * jnp.arange(USERS, dtype=jnp.float32) / (USERS - 1)
    return (base * ramp).astype(jnp.bfloat16)


def setup_inputs(seed: int = 0) -> dict:
    key_list = jax.random.split(jax.random.key(seed), 4)
    return {
        "interactions": draw_interactions(jax.random.fold_in(key_list[3], 71), 0),
        "user_weights": draw_user_weights(jax.random.fold_in(key_list[3], 71), 0),
        "panel_index": jax.random.randint(key_list[2], (1,), 0, N // P_SIZE).astype(jnp.int32),
    }


def reference(interactions, user_weights, panel_index):
    start = panel_index[0].astype(jnp.int32) * P_SIZE
    panel = lax.dynamic_slice_in_dim(interactions, start, P_SIZE, 1)
    weights32 = user_weights.astype(jnp.float32)
    weighted = (weights32[:, None] * panel.astype(jnp.float32)).astype(jnp.bfloat16)
    blocks = interactions.reshape(N_USERS, USR_DEV, N)
    weighted_blocks = weighted.reshape(N_USERS, USR_DEV, P_SIZE)
    weight_blocks = user_weights.reshape(N_USERS, USR_DEV)

    def accumulate(carry, pieces):
        gram, colsum = carry
        block, wpanel, wrow = pieces
        dense = block.astype(jnp.float32)
        gram = gram + jnp.dot(dense.T, wpanel.astype(jnp.float32))
        colsum = colsum + jnp.dot(wrow.astype(jnp.float32), dense)
        return (gram, colsum), None

    start_carry = (jnp.zeros((N, P_SIZE), jnp.float32), jnp.zeros((N,), jnp.float32))
    (gram, colsum), _ = lax.scan(accumulate, start_carry, (blocks, weighted_blocks, weight_blocks))
    count = jnp.sum(weights32)
    panel_sum = jnp.dot(weights32, panel.astype(jnp.float32))
    mean = colsum / count
    panel_mean = panel_sum / count
    covariance = gram / count - mean[:, None] * panel_mean[None, :]
    width = BLK * N_USERS * N_ITEMS
    return covariance.reshape(CYC, width, P_SIZE), mean.reshape(CYC, width)
```

```python
import functools
import math

import jax
import jax.numpy as jnp
from jax import lax
from jax.experimental import pallas as pl
from jax.experimental.pallas import tpu as pltpu
from jax.sharding import PartitionSpec as P

P_SIZE = 256
BLK = 32
EXTRA = 16
TILE = 256
PIECES = 4
LAG = 3
STEP = math.log(2.0) / 256.0
TOP = 32600.0
f32 = jnp.float32


def encode(block):
    top = jnp.max(jnp.abs(block), axis=0, keepdims=True)
    code = jnp.ceil(jnp.log(jnp.maximum(top, 1e-30)) * (1.0 / STEP)) + 1.0
    scaled = jnp.round(block * (jnp.exp(code * -STEP) * TOP))
    codes = jnp.broadcast_to(code, (EXTRA, block.shape[1]))
    return scaled.astype(jnp.int32).astype(jnp.int16), codes.astype(jnp.int32).astype(jnp.int16)


def decode(ref):
    code = ref[P_SIZE : P_SIZE + EXTRA, :].astype(jnp.int32).astype(f32)[0:1]
    return ref[0:P_SIZE, :].astype(jnp.int32).astype(f32) * (jnp.exp(code * STEP) * (1.0 / TOP))


def kernel(
    sizes, x_ref, loc_ref, w_ref, cov_ref, mean_ref,
    xbuf, turned, full, half, near, far, lhs, pmean, gram, own,
    xsend, xrecv, zsend, zrecv, icov, sums, sums_all, stat, stat_all, shift, mean_mine, mean_all,
    load_sem, near_s, near_r, far_s, far_r, back_s, back_r, xs, xr, zs, zr, is_, ir,
    sum_s, sum_r, stat_s, stat_r, mean_s, mean_r,
):
    users, items, xn, zn, cyc, width = sizes
    rows = loc_ref.shape[0]
    chunk = users * width
    user, item = lax.axis_index("users"), lax.axis_index("items")
    z, x = lax.div(user, xn), lax.rem(user, xn)
    y, core = lax.div(item, 2), lax.rem(item, 2)
    yn = items // 2

    def load(c):
        return pltpu.make_async_copy(x_ref.at[:, pl.ds(c * chunk, chunk)], xbuf.at[c], load_sem.at[c])

    def remote(src, dst, send, recv, to_user, to_item):
        return pltpu.make_async_remote_copy(
            src_ref=src, dst_ref=dst, send_sem=send, recv_sem=recv,
            device_id={"users": to_user, "items": to_item},
            device_id_type=pl.DeviceIdType.MESH,
        )

    for c in range(cyc):
        load(c).start()

    barrier = pltpu.get_barrier_semaphore()
    for d in range(1, users):
        pl.semaphore_signal(
            barrier, inc=1, device_id={"users": lax.rem(user + d, users), "items": item},
            device_id_type=pl.DeviceIdType.MESH,
        )
    for d in range(1, items):
        pl.semaphore_signal(
            barrier, inc=1, device_id={"users": user, "items": lax.rem(item + d, items)},
            device_id_type=pl.DeviceIdType.MESH,
        )
    for r in range(rows // TILE):
        part = pl.ds(r * TILE, TILE)
        turned[:, part] = loc_ref[part, :].astype(f32).T.astype(jnp.bfloat16)
    pl.semaphore_wait(barrier, users + items - 2)

    side = P_SIZE // 2
    piece = side // PIECES

    def near_copy(p):
        start = pl.multiple_of((1 - core) * side + p * piece, piece)
        return remote(turned.at[pl.ds(start, piece)], near.at[pl.ds(p * piece, piece)],
                      near_s.at[p], near_r.at[p], user, y * 2 + 1 - core)

    def far_copy(p, d):
        return remote(half.at[pl.ds(p * piece, piece)], far.at[d - 1, pl.ds(p * piece, piece)],
                      far_s.at[p, d - 1], far_r.at[p, d - 1], user, lax.rem(y + d, yn) * 2 + core)

    def back_copy(p):
        start = pl.multiple_of(core * side + p * piece, piece)
        return remote(full.at[pl.ds(start, piece)], full.at[pl.ds(start, piece)],
                      back_s.at[p], back_r.at[p], user, y * 2 + 1 - core)

    for p in range(PIECES):
        near_copy(p).start()
    for p in range(PIECES):
        near_copy(p).wait_recv()
        mine = pl.ds(pl.multiple_of(core * side + p * piece, piece), piece)
        here = pl.ds(p * piece, piece)
        half[here, :] = turned[mine, :] + near[here, :]
        for d in range(1, yn):
            far_copy(p, d).start()
    for p in range(PIECES):
        here = pl.ds(p * piece, piece)
        value = half[here, :]
        for d in range(1, yn):
            far_copy(p, d).wait_recv()
            value = value + far[d - 1, here, :]
        full[pl.ds(pl.multiple_of(core * side + p * piece, piece), piece), :] = value
        back_copy(p).start()
    for p in range(PIECES):
        back_copy(p).wait_recv()

    weights = w_ref[...]
    count = jnp.sum(weights, axis=1, keepdims=True)
    for r in range(P_SIZE // 64):
        part = pl.ds(r * 64, 64)
        product = full[part, :].astype(f32) * weights
        lhs[part, :] = product.astype(jnp.bfloat16)
        pmean[part, :] = jnp.broadcast_to(jnp.sum(product, axis=1, keepdims=True), (64, 128))
    lhs[P_SIZE : P_SIZE + EXTRA, :] = jnp.broadcast_to(weights, (EXTRA, rows)).astype(jnp.bfloat16)
    stat[0:8, :] = pmean[...].T[0:8, :]
    stat[8:16, :] = jnp.broadcast_to(count, (8, P_SIZE))
    pmean[...] = pmean[...] / count

    def stat_copy(d):
        return remote(stat, stat_all.at[user], stat_s.at[d - 1], stat_r.at[d - 1],
                      lax.rem(user + d, users), item)

    for d in range(1, users):
        stat_copy(d).start()

    def x_copy(c, d):
        return remote(xsend.at[c, d - 1], xrecv.at[c, d - 1], xs.at[c, d - 1], xr.at[c, d - 1],
                      z * xn + lax.rem(x + d, xn), item)

    def z_copy(c, d):
        return remote(zsend.at[c, d - 1], zrecv.at[c, d - 1], zs.at[c, d - 1], zr.at[c, d - 1],
                      lax.rem(z + d, zn) * xn + x, item)

    def item_copy(c, d):
        peer = lax.rem(item + d, items)
        return remote(icov.at[c, pl.ds(pl.multiple_of(peer * BLK, BLK), BLK)],
                      cov_ref.at[item * cyc + c],
                      is_.at[c, d - 1], ir.at[c, d - 1], user, peer)

    def compute(c):
        load(c).wait()

        def tile(t, _):
            part = pl.ds(pl.multiple_of(t * TILE, TILE), TILE)
            value = jnp.dot(lhs[...], xbuf[c, :, part], preferred_element_type=f32)
            total = value[P_SIZE : P_SIZE + 1, :]
            gram[:, part] = value[0:P_SIZE, :] - pmean[:, 0:1] * total
            for b in range(TILE // width):
                sums[t * (TILE // width) + b, pl.ds(c, 1), :] = total[:, b * width : (b + 1) * width]
            return 0

        lax.fori_loop(0, chunk // TILE, tile, 0)
        for d in range(1, xn):
            for k in range(zn):
                start = pl.multiple_of((k * xn + lax.rem(x + d, xn)) * width, width)
                part = pl.ds(k * width, width)
                codes, scales = encode(gram[:, pl.ds(start, width)])
                xsend[c, d - 1, 0:P_SIZE, part] = codes
                xsend[c, d - 1, P_SIZE : P_SIZE + EXTRA, part] = scales
            x_copy(c, d).start()
        for k in range(zn):
            start = pl.multiple_of((k * xn + x) * width, width)
            own[c, :, pl.ds(k * width, width)] = gram[:, pl.ds(start, width)]

    def relay(c):
        for d in range(1, xn):
            x_copy(c, d).wait_recv()
            own[c] = own[c] + decode(xrecv.at[c, d - 1])
        for d in range(1, zn):
            start = pl.multiple_of(lax.rem(z + d, zn) * width, width)
            codes, scales = encode(own[c, :, pl.ds(start, width)])
            zsend[c, d - 1, 0:P_SIZE, :] = codes
            zsend[c, d - 1, P_SIZE : P_SIZE + EXTRA, :] = scales
            z_copy(c, d).start()

    lag = min(LAG, cyc)

    def first(c, _):
        compute(c)

        @pl.when(c >= lag)
        def _():
            relay(c - lag)

        return 0

    lax.fori_loop(0, cyc, first, 0)

    def sum_copy(d):
        peer = lax.rem(user + d, users)
        return remote(sums.at[peer], sums_all.at[user], sum_s.at[d - 1], sum_r.at[d - 1], peer, item)

    for d in range(1, users):
        sum_copy(d).start()
    sums_all[user] = sums[user]
    stat_all[user] = stat[...]
    for d in range(1, users):
        stat_copy(d).wait_recv()
    whole = stat_all[0]
    for g in range(1, users):
        whole = whole + stat_all[g]
    total = whole[8:9, 0:1]
    panel_mean = whole[0:1, :] / whole[8:9, :]
    for g in range(users):
        delta = stat_all[g, 0:1, :] / stat_all[g, 8:9, :] - panel_mean
        shift[g] = jnp.broadcast_to(delta, (width, P_SIZE)).T
    for d in range(1, users):
        sum_copy(d).wait_recv()
    means = sums_all[0]
    for g in range(1, users):
        means = means + sums_all[g]
    mean_mine[...] = means / total

    def mean_copy(d):
        return remote(mean_mine, mean_all.at[item], mean_s.at[d - 1], mean_r.at[d - 1],
                      user, lax.rem(item + d, items))

    for d in range(1, items):
        mean_copy(d).start()
    mean_all[item] = mean_mine[...]

    def finish(c):
        value = own[c, :, pl.ds(pl.multiple_of(z * width, width), width)]
        for g in range(users):
            value = value + shift[g] * sums_all[g, pl.ds(c, 1), :]
        for d in range(1, zn):
            z_copy(c, d).wait_recv()
            value = value + decode(zrecv.at[c, d - 1])
        icov[c] = (value / total).T
        for d in range(1, items):
            item_copy(c, d).start()
        cov_ref[item * cyc + c] = icov[c, pl.ds(pl.multiple_of(item * BLK, BLK), BLK), :]

    def second(c, _):
        @pl.when(c < lag)
        def _():
            relay(cyc - lag + c)

        finish(c)
        return 0

    lax.fori_loop(0, cyc, second, 0)

    for d in range(1, items):
        mean_copy(d).wait()
    for i in range(items):
        value = jnp.zeros(mean_ref.shape[1:], f32)
        for k in range(items):
            value = jnp.where(item == k, mean_all[i, :, k * BLK : (k + 1) * BLK], value)
        mean_ref[i] = value

    for p in range(PIECES):
        near_copy(p).wait_send()
        back_copy(p).wait_send()
        for d in range(1, yn):
            far_copy(p, d).wait_send()
    for d in range(1, users):
        stat_copy(d).wait_send()
        sum_copy(d).wait_send()

    def drain(c, _):
        for d in range(1, xn):
            x_copy(c, d).wait_send()
        for d in range(1, zn):
            z_copy(c, d).wait_send()
        for d in range(1, items):
            item_copy(c, d).wait()
        return 0

    lax.fori_loop(0, cyc, drain, 0)


def per_device(interactions, user_weights, panel_index):
    rows, shard = interactions.shape
    users, items = lax.axis_size("users"), lax.axis_size("items")
    zn = 4 if users % 4 == 0 else 1
    xn = users // zn
    width = items * BLK
    cyc = shard // (users * width)
    cyc8 = -(-cyc // 8) * 8
    yn = items // 2
    per_shard = shard // P_SIZE
    chosen = panel_index[0]
    local = lax.dynamic_slice_in_dim(interactions, chosen % per_shard * P_SIZE, P_SIZE, 1)
    local = jnp.where(lax.axis_index("items") == chosen // per_shard, local, jnp.zeros_like(local))
    weights = user_weights.astype(f32)[None, :]

    bf16, i16 = jnp.bfloat16, jnp.int16
    side, tall = P_SIZE // 2, P_SIZE + EXTRA
    dma = pltpu.SemaphoreType.DMA
    vmem = pl.BlockSpec(memory_space=pltpu.VMEM)
    cov, mean = pl.pallas_call(
        functools.partial(kernel, (users, items, xn, zn, cyc, width)),
        out_shape=(
            jax.ShapeDtypeStruct((items * cyc, BLK, P_SIZE), f32),
            jax.ShapeDtypeStruct((items, cyc8, BLK), f32),
        ),
        in_specs=[pl.BlockSpec(memory_space=pl.ANY), vmem, vmem],
        out_specs=(vmem, vmem),
        scratch_shapes=[
            pltpu.VMEM((cyc, rows, users * width), bf16),
            pltpu.VMEM((P_SIZE, rows), bf16),
            pltpu.VMEM((P_SIZE, rows), bf16),
            pltpu.VMEM((side, rows), bf16),
            pltpu.VMEM((side, rows), bf16),
            pltpu.VMEM((yn - 1, side, rows), bf16),
            pltpu.VMEM((tall, rows), bf16),
            pltpu.VMEM((P_SIZE, 128), f32),
            pltpu.VMEM((P_SIZE, users * width), f32),
            pltpu.VMEM((cyc, P_SIZE, zn * width), f32),
            pltpu.VMEM((cyc, xn - 1, tall, zn * width), i16),
            pltpu.VMEM((cyc, xn - 1, tall, zn * width), i16),
            pltpu.VMEM((cyc, zn - 1, tall, width), i16),
            pltpu.VMEM((cyc, zn - 1, tall, width), i16),
            pltpu.VMEM((cyc, width, P_SIZE), f32),
            pltpu.VMEM((users, cyc8, width), f32),
            pltpu.VMEM((users, cyc8, width), f32),
            pltpu.VMEM((16, P_SIZE), f32),
            pltpu.VMEM((users, 16, P_SIZE), f32),
            pltpu.VMEM((users, P_SIZE, width), f32),
            pltpu.VMEM((cyc8, width), f32),
            pltpu.VMEM((items, cyc8, width), f32),
            dma((cyc,)),
            dma((PIECES,)), dma((PIECES,)),
            dma((PIECES, yn - 1)), dma((PIECES, yn - 1)),
            dma((PIECES,)), dma((PIECES,)),
            dma((cyc, xn - 1)), dma((cyc, xn - 1)),
            dma((cyc, zn - 1)), dma((cyc, zn - 1)),
            dma((cyc, items - 1)), dma((cyc, items - 1)),
            dma((users - 1,)), dma((users - 1,)),
            dma((users - 1,)), dma((users - 1,)),
            dma((items - 1,)), dma((items - 1,)),
        ],
        compiler_params=pltpu.CompilerParams(
            collective_id=0, has_side_effects=True, vmem_limit_bytes=60 * 2**20
        ),
        cost_estimate=pl.CostEstimate(
            flops=2 * tall * rows * shard, bytes_accessed=2 * rows * shard, transcendentals=0
        ),
        name="panel_covariance",
    )(interactions, local, weights)
    return cov, mean[:, :cyc].reshape(items * cyc, BLK)


def solution(mesh):
    return jax.shard_map(
        per_device,
        mesh=mesh,
        in_specs=(P("users", "items"), P("users"), P()),
        out_specs=(P(None, ("users", "items"), None), P(None, ("users", "items"))),
        check_vma=False,
    )
```

```python
import functools
import math

import jax
import jax.numpy as jnp
from jax import lax
from jax.experimental import pallas as pl
from jax.experimental.pallas import tpu as pltpu
from jax.sharding import PartitionSpec as P

P_SIZE = 256
BLK = 32
EXTRA = 16
TILE = 256
PHASES = 2
COLS = P_SIZE // PHASES
PIECES = 2
LAG = 3
STEP = math.log(2.0) / 256.0
TOP = 32600.0
f32 = jnp.float32


def encode(block):
    top = jnp.max(jnp.abs(block), axis=0, keepdims=True)
    code = jnp.ceil(jnp.log(jnp.maximum(top, 1e-30)) * (1.0 / STEP)) + 1.0
    scaled = jnp.round(block * (jnp.exp(code * -STEP) * TOP))
    return scaled.astype(jnp.int32).astype(jnp.int16), code


def decode(codes, code):
    return codes.astype(jnp.int32).astype(f32) * (jnp.exp(code * STEP) * (1.0 / TOP))


def kernel(
    sizes, x_ref, loc_ref, w_ref, cov_ref, mean_ref,
    xbuf, turned, full, half, near, far, lhs, pmean, gram, own,
    xsend, xrecv, zsend, zrecv, icov, sums, sums_all, stat, stat_all, shift, mean_mine, mean_all,
    load_sem, near_s, near_r, far_s, far_r, back_s, back_r, xs, xr, zs, zr, is_, ir,
    sum_s, sum_r, stat_s, stat_r, mean_s, mean_r,
):
    users, items, xn, zn, cyc, width = sizes
    rows = loc_ref.shape[0]
    chunk = users * width
    user, item = lax.axis_index("users"), lax.axis_index("items")
    z, x = lax.div(user, xn), lax.rem(user, xn)
    y, core = lax.div(item, 2), lax.rem(item, 2)
    yn = items // 2
    units = PHASES * cyc

    def load(c):
        return pltpu.make_async_copy(x_ref.at[:, pl.ds(c * chunk, chunk)], xbuf.at[c], load_sem.at[c])

    def remote(src, dst, send, recv, to_user, to_item):
        return pltpu.make_async_remote_copy(
            src_ref=src, dst_ref=dst, send_sem=send, recv_sem=recv,
            device_id={"users": to_user, "items": to_item},
            device_id_type=pl.DeviceIdType.MESH,
        )

    for c in range(cyc):
        load(c).start()

    barrier = pltpu.get_barrier_semaphore()
    for d in range(1, users):
        pl.semaphore_signal(
            barrier, inc=1, device_id={"users": lax.rem(user + d, users), "items": item},
            device_id_type=pl.DeviceIdType.MESH,
        )
    for d in range(1, items):
        pl.semaphore_signal(
            barrier, inc=1, device_id={"users": user, "items": lax.rem(item + d, items)},
            device_id_type=pl.DeviceIdType.MESH,
        )
    for r in range(rows // TILE):
        part = pl.ds(r * TILE, TILE)
        turned[:, part] = loc_ref[part, :].astype(f32).T.astype(jnp.bfloat16)
    pl.semaphore_wait(barrier, users + items - 2)

    side = COLS // 2
    piece = side // PIECES

    def place(f, p, whose):
        return pl.ds(pl.multiple_of(f * COLS + whose * side + p * piece, piece), piece)

    def near_copy(f, p):
        n = f * PIECES + p
        return remote(turned.at[place(f, p, 1 - core)], near.at[n],
                      near_s.at[n], near_r.at[n], user, y * 2 + 1 - core)

    def far_copy(f, p, d):
        n = f * PIECES + p
        return remote(half.at[n], far.at[n, d - 1], far_s.at[n, d - 1], far_r.at[n, d - 1],
                      user, lax.rem(y + d, yn) * 2 + core)

    def back_copy(f, p):
        n = f * PIECES + p
        return remote(full.at[place(f, p, core)], full.at[place(f, p, core)],
                      back_s.at[n], back_r.at[n], user, y * 2 + 1 - core)

    def panel_back(f):
        for p in range(PIECES):
            value = half[f * PIECES + p]
            for d in range(1, yn):
                far_copy(f, p, d).wait_recv()
                value = value + far[f * PIECES + p, d - 1]
            full[place(f, p, core), :] = value
            back_copy(f, p).start()

    def panel_weigh(f):
        for p in range(PIECES):
            back_copy(f, p).wait_recv()
        weights = jnp.concatenate([w_ref[r : r + 1, :] for r in range(rows // 128)], axis=1).astype(f32)
        count = jnp.sum(weights, axis=1, keepdims=True)
        for r in range(0, COLS, 64):
            part = pl.ds(f * COLS + r, 64)
            product = full[part, :].astype(f32) * weights
            lhs[f, r : r + 64, :] = product.astype(jnp.bfloat16)
            pmean[part, :] = jnp.broadcast_to(jnp.sum(product, axis=1, keepdims=True), (64, 128))
        lhs[f, COLS : COLS + EXTRA, :] = jnp.broadcast_to(weights, (EXTRA, rows)).astype(jnp.bfloat16)
        part = pl.ds(f * COLS, COLS)
        stat[0:8, part] = pmean[part, :].T[0:8, :]
        stat[8:16, part] = jnp.broadcast_to(count, (8, COLS))
        pmean[part, :] = pmean[part, :] / count

    for f in range(PHASES):
        for p in range(PIECES):
            near_copy(f, p).start()
    for f in range(PHASES):
        for p in range(PIECES):
            near_copy(f, p).wait_recv()
            half[f * PIECES + p] = turned[place(f, p, core), :] + near[f * PIECES + p]
            for d in range(1, yn):
                far_copy(f, p, d).start()
    panel_back(0)
    panel_weigh(0)

    def stat_copy(d):
        return remote(stat, stat_all.at[user], stat_s.at[d - 1], stat_r.at[d - 1],
                      lax.rem(user + d, users), item)

    def sum_copy(d):
        peer = lax.rem(user + d, users)
        return remote(sums.at[peer], sums_all.at[user], sum_s.at[d - 1], sum_r.at[d - 1], peer, item)

    def mean_copy(d):
        return remote(mean_mine, mean_all.at[item], mean_s.at[d - 1], mean_r.at[d - 1],
                      user, lax.rem(item + d, items))

    def x_copy(n, d):
        return remote(xsend.at[n, d - 1], xrecv.at[n, d - 1], xs.at[n, d - 1], xr.at[n, d - 1],
                      z * xn + lax.rem(x + d, xn), item)

    def z_copy(n, d):
        return remote(zsend.at[n, d - 1], zrecv.at[n, d - 1], zs.at[n, d - 1], zr.at[n, d - 1],
                      lax.rem(z + d, zn) * xn + x, item)

    def item_copy(n, d):
        peer = lax.rem(item + d, items)
        f, c = lax.div(n, cyc), lax.rem(n, cyc)
        return remote(icov.at[n, pl.ds(pl.multiple_of(peer * BLK, BLK), BLK)],
                      cov_ref.at[item * cyc + c, :, pl.ds(pl.multiple_of(f * COLS, COLS), COLS)],
                      is_.at[n, d - 1], ir.at[n, d - 1], user, peer)

    def compute(n):
        f, c = lax.div(n, cyc), lax.rem(n, cyc)

        @pl.when(f == 0)
        def _():
            load(c).wait()

        mean = pmean[pl.ds(pl.multiple_of(f * COLS, COLS), COLS), 0:1]

        def tile(t, _):
            part = pl.ds(pl.multiple_of(t * TILE, TILE), TILE)
            value = jnp.dot(lhs[f], xbuf[c, :, part], preferred_element_type=f32)
            total = value[COLS : COLS + 1, :]
            gram[:, part] = value[0:COLS, :] - mean * total

            @pl.when(f == 0)
            def _():
                for b in range(TILE // width):
                    sums[t * (TILE // width) + b, pl.ds(c, 1), :] = total[:, b * width : (b + 1) * width]

            return 0

        lax.fori_loop(0, chunk // TILE, tile, 0)
        row = lax.broadcasted_iota(jnp.int32, (EXTRA, width), 0)
        for d in range(1, xn):
            scales = jnp.zeros((EXTRA, width), f32)
            for k in range(zn):
                start = pl.multiple_of((k * xn + lax.rem(x + d, xn)) * width, width)
                codes, code = encode(gram[:, pl.ds(start, width)])
                xsend[n, d - 1, k * COLS : (k + 1) * COLS, :] = codes
                scales = jnp.where(row == k, code, scales)
            xsend[n, d - 1, zn * COLS : zn * COLS + EXTRA, :] = scales.astype(jnp.int32).astype(jnp.int16)
            x_copy(n, d).start()
        for k in range(zn):
            start = pl.multiple_of((k * xn + x) * width, width)
            own[n, k] = gram[:, pl.ds(start, width)]

    def relay(n):
        for d in range(1, xn):
            x_copy(n, d).wait_recv()
            scales = xrecv[n, d - 1, zn * COLS : zn * COLS + EXTRA, :].astype(jnp.int32).astype(f32)
            for k in range(zn):
                codes = xrecv[n, d - 1, k * COLS : (k + 1) * COLS, :]
                own[n, k] = own[n, k] + decode(codes, scales[k : k + 1])
        for d in range(1, zn):
            codes, code = encode(own[n, lax.rem(z + d, zn)])
            zsend[n, d - 1, 0:COLS, :] = codes
            code = jnp.broadcast_to(code, (EXTRA, width))
            zsend[n, d - 1, COLS : COLS + EXTRA, :] = code.astype(jnp.int32).astype(jnp.int16)
            z_copy(n, d).start()

    def statistics():
        sums_all[user] = sums[user]
        stat_all[user] = stat[...]
        for d in range(1, users):
            stat_copy(d).wait_recv()
        whole = stat_all[0]
        for g in range(1, users):
            whole = whole + stat_all[g]
        panel_mean = whole[0:1, :] / whole[8:9, :]
        for g in range(users):
            delta = stat_all[g, 0:1, :] / stat_all[g, 8:9, :] - panel_mean
            shift[g] = jnp.broadcast_to(delta, (width, P_SIZE)).T
        for d in range(1, users):
            sum_copy(d).wait_recv()
        means = sums_all[0]
        for g in range(1, users):
            means = means + sums_all[g]
        mean_mine[...] = means / whole[8:9, 0:1]
        for d in range(1, items):
            mean_copy(d).start()
        mean_all[item] = mean_mine[...]

    def finish(n):
        f, c = lax.div(n, cyc), lax.rem(n, cyc)
        value = own[n, z]
        for g in range(users):
            part = pl.ds(pl.multiple_of(f * COLS, COLS), COLS)
            value = value + shift[g, part, :] * sums_all[g, pl.ds(c, 1), :]
        for d in range(1, zn):
            z_copy(n, d).wait_recv()
            code = zrecv[n, d - 1, COLS : COLS + EXTRA, :].astype(jnp.int32).astype(f32)[0:1]
            value = value + decode(zrecv[n, d - 1, 0:COLS, :], code)
        total = stat_all[0, 8:9, 0:1]
        for g in range(1, users):
            total = total + stat_all[g, 8:9, 0:1]
        icov[n] = (value / total).T
        for d in range(1, items):
            item_copy(n, d).start()
        part = pl.ds(pl.multiple_of(f * COLS, COLS), COLS)
        cov_ref[item * cyc + c, :, part] = icov[n, pl.ds(pl.multiple_of(item * BLK, BLK), BLK), :]

    lag = min(LAG, units)
    last = cyc + lag

    def step(s, _):
        @pl.when(s < units)
        def _():
            compute(s)

        @pl.when(s == min(1, cyc - 1))
        def _():
            for f in range(1, PHASES):
                panel_back(f)

        @pl.when(s == min(3, cyc - 1))
        def _():
            for f in range(1, PHASES):
                panel_weigh(f)
            for d in range(1, users):
                stat_copy(d).start()

        @pl.when(s == cyc - 1)
        def _():
            for d in range(1, users):
                sum_copy(d).start()

        @pl.when(s >= lag)
        def _():
            relay(s - lag)

        @pl.when(s == last)
        def _():
            statistics()

        @pl.when(s >= last)
        def _():
            for k in range(PHASES):
                finish((s - last) * PHASES + k)

        return 0

    lax.fori_loop(0, units + lag, step, 0)

    for d in range(1, items):
        mean_copy(d).wait()
    for i in range(items):
        value = jnp.zeros((mean_all.shape[1], BLK), f32)
        for k in range(items):
            value = jnp.where(item == k, mean_all[i, :, k * BLK : (k + 1) * BLK], value)
        mean_ref[i * cyc : (i + 1) * cyc, :] = value[0:cyc]

    for f in range(PHASES):
        for p in range(PIECES):
            near_copy(f, p).wait_send()
            back_copy(f, p).wait_send()
            for d in range(1, yn):
                far_copy(f, p, d).wait_send()
    for d in range(1, users):
        stat_copy(d).wait_send()
        sum_copy(d).wait_send()

    def drain(n, _):
        for d in range(1, xn):
            x_copy(n, d).wait_send()
        for d in range(1, zn):
            z_copy(n, d).wait_send()
        for d in range(1, items):
            item_copy(n, d).wait()
        return 0

    lax.fori_loop(0, units, drain, 0)


def per_device(interactions, user_weights, panel_index):
    rows, shard = interactions.shape
    users, items = lax.axis_size("users"), lax.axis_size("items")
    zn = 4 if users % 4 == 0 else 1
    xn = users // zn
    width = items * BLK
    cyc = shard // (users * width)
    cyc8 = -(-cyc // 8) * 8
    yn = items // 2
    per_shard = shard // P_SIZE
    chosen = panel_index[0]
    local = lax.dynamic_slice_in_dim(interactions, chosen % per_shard * P_SIZE, P_SIZE, 1)
    local = jnp.where(lax.axis_index("items") == chosen // per_shard, local, jnp.zeros_like(local))
    weights = user_weights.reshape(rows // 128, 128)

    bf16, i16 = jnp.bfloat16, jnp.int16
    piece, tall = COLS // 2 // PIECES, COLS + EXTRA
    pieces, units = PHASES * PIECES, PHASES * cyc
    dma = pltpu.SemaphoreType.DMA
    vmem = pl.BlockSpec(memory_space=pltpu.VMEM)
    cov, mean = pl.pallas_call(
        functools.partial(kernel, (users, items, xn, zn, cyc, width)),
        out_shape=(
            jax.ShapeDtypeStruct((items * cyc, BLK, P_SIZE), f32),
            jax.ShapeDtypeStruct((items * cyc, BLK), f32),
        ),
        in_specs=[pl.BlockSpec(memory_space=pl.ANY), vmem, vmem],
        out_specs=(vmem, vmem),
        scratch_shapes=[
            pltpu.VMEM((cyc, rows, users * width), bf16),
            pltpu.VMEM((P_SIZE, rows), bf16),
            pltpu.VMEM((P_SIZE, rows), bf16),
            pltpu.VMEM((pieces, piece, rows), bf16),
            pltpu.VMEM((pieces, piece, rows), bf16),
            pltpu.VMEM((pieces, yn - 1, piece, rows), bf16),
            pltpu.VMEM((PHASES, tall, rows), bf16),
            pltpu.VMEM((P_SIZE, 128), f32),
            pltpu.VMEM((COLS, users * width), f32),
            pltpu.VMEM((units, zn, COLS, width), f32),
            pltpu.VMEM((units, xn - 1, zn * COLS + EXTRA, width), i16),
            pltpu.VMEM((units, xn - 1, zn * COLS + EXTRA, width), i16),
            pltpu.VMEM((units, zn - 1, tall, width), i16),
            pltpu.VMEM((units, zn - 1, tall, width), i16),
            pltpu.VMEM((units, width, COLS), f32),
            pltpu.VMEM((users, cyc8, width), f32),
            pltpu.VMEM((users, cyc8, width), f32),
            pltpu.VMEM((16, P_SIZE), f32),
            pltpu.VMEM((users, 16, P_SIZE), f32),
            pltpu.VMEM((users, P_SIZE, width), f32),
            pltpu.VMEM((cyc8, width), f32),
            pltpu.VMEM((items, cyc8, width), f32),
            dma((cyc,)),
            dma((pieces,)), dma((pieces,)),
            dma((pieces, yn - 1)), dma((pieces, yn - 1)),
            dma((pieces,)), dma((pieces,)),
            dma((units, xn - 1)), dma((units, xn - 1)),
            dma((units, zn - 1)), dma((units, zn - 1)),
            dma((units, items - 1)), dma((units, items - 1)),
            dma((users - 1,)), dma((users - 1,)),
            dma((users - 1,)), dma((users - 1,)),
            dma((items - 1,)), dma((items - 1,)),
        ],
        compiler_params=pltpu.CompilerParams(
            collective_id=0, has_side_effects=True, vmem_limit_bytes=60 * 2**20
        ),
        cost_estimate=pl.CostEstimate(
            flops=2 * P_SIZE * rows * shard, bytes_accessed=2 * rows * shard, transcendentals=0
        ),
        name="panel_covariance",
    )(interactions, local, weights)
    return cov, mean


def solution(mesh):
    return jax.shard_map(
        per_device,
        mesh=mesh,
        in_specs=(P("users", "items"), P("users"), P()),
        out_specs=(P(None, ("users", "items"), None), P(None, ("users", "items"))),
        check_vma=False,
    )
```

```python
import functools
import math

import jax
import jax.numpy as jnp
from jax import lax
from jax.experimental import pallas as pl
from jax.experimental.pallas import tpu as pltpu
from jax.sharding import PartitionSpec as P

P_SIZE = 256
BLK = 32
EXTRA = 16
TILE = 256
DOT = 1024
PHASES = 2
COLS = P_SIZE // PHASES
PIECES = 2
LAG = 3
STEP = math.log(2.0) / 256.0
TOP = 32600.0
f32 = jnp.float32


def encode(block):
    top = jnp.max(jnp.abs(block), axis=0, keepdims=True)
    code = jnp.ceil(jnp.log(jnp.maximum(top, 1e-30)) * (1.0 / STEP)) + 1.0
    scaled = jnp.round(block * (jnp.exp(code * -STEP) * TOP))
    return scaled.astype(jnp.int32).astype(jnp.int16), code


def decode(codes, code):
    return codes.astype(jnp.int32).astype(f32) * (jnp.exp(code * STEP) * (1.0 / TOP))


def kernel(
    sizes, x_ref, loc_ref, w_ref, cov_ref, mean_ref,
    xbuf, turned, full, half, near, far, lhs, pmean, gram, own,
    xsend, xrecv, zsend, zrecv, icov, sums, sums_all, stat, stat_all, shift, mean_mine, mean_all,
    load_sem, near_s, near_r, far_s, far_r, back_s, back_r, xs, xr, zs, zr, is_, ir,
    sum_s, sum_r, stat_s, stat_r, mean_s, mean_r,
):
    users, items, xn, zn, cyc, width = sizes
    rows = loc_ref.shape[0]
    chunk = users * width
    user, item = lax.axis_index("users"), lax.axis_index("items")
    z, x = lax.div(user, xn), lax.rem(user, xn)
    y, core = lax.div(item, 2), lax.rem(item, 2)
    yn = items // 2
    units = PHASES * cyc

    def load(c):
        return pltpu.make_async_copy(x_ref.at[:, pl.ds(c * chunk, chunk)], xbuf.at[c], load_sem.at[c])

    def remote(src, dst, send, recv, to_user, to_item):
        return pltpu.make_async_remote_copy(
            src_ref=src, dst_ref=dst, send_sem=send, recv_sem=recv,
            device_id={"users": to_user, "items": to_item},
            device_id_type=pl.DeviceIdType.MESH,
        )

    for c in range(cyc):
        load(c).start()

    barrier = pltpu.get_barrier_semaphore()
    for d in range(1, users):
        pl.semaphore_signal(
            barrier, inc=1, device_id={"users": lax.rem(user + d, users), "items": item},
            device_id_type=pl.DeviceIdType.MESH,
        )
    for d in range(1, items):
        pl.semaphore_signal(
            barrier, inc=1, device_id={"users": user, "items": lax.rem(item + d, items)},
            device_id_type=pl.DeviceIdType.MESH,
        )
    for r in range(rows // TILE):
        part = pl.ds(r * TILE, TILE)
        turned[:, part] = loc_ref[part, :].astype(f32).T.astype(jnp.bfloat16)
    pl.semaphore_wait(barrier, users + items - 2)

    side = COLS // 2
    piece = side // PIECES

    def place(f, p, whose):
        return pl.ds(pl.multiple_of(f * COLS + whose * side + p * piece, piece), piece)

    def near_copy(f, p):
        n = f * PIECES + p
        return remote(turned.at[place(f, p, 1 - core)], near.at[n],
                      near_s.at[n], near_r.at[n], user, y * 2 + 1 - core)

    def far_copy(f, p, d):
        n = f * PIECES + p
        return remote(half.at[n], far.at[n, d - 1], far_s.at[n, d - 1], far_r.at[n, d - 1],
                      user, lax.rem(y + d, yn) * 2 + core)

    def back_copy(f, p):
        n = f * PIECES + p
        return remote(full.at[place(f, p, core)], full.at[place(f, p, core)],
                      back_s.at[n], back_r.at[n], user, y * 2 + 1 - core)

    def panel_back(f):
        for p in range(PIECES):
            value = half[f * PIECES + p]
            for d in range(1, yn):
                far_copy(f, p, d).wait_recv()
                value = value + far[f * PIECES + p, d - 1]
            full[place(f, p, core), :] = value
            back_copy(f, p).start()

    def panel_weigh(f):
        for p in range(PIECES):
            back_copy(f, p).wait_recv()
        weights = jnp.concatenate([w_ref[r : r + 1, :] for r in range(rows // 128)], axis=1).astype(f32)
        count = jnp.sum(weights, axis=1, keepdims=True)
        for r in range(0, COLS, 64):
            part = pl.ds(f * COLS + r, 64)
            product = full[part, :].astype(f32) * weights
            lhs[f, r : r + 64, :] = product.astype(jnp.bfloat16)
            pmean[part, :] = jnp.broadcast_to(jnp.sum(product, axis=1, keepdims=True), (64, 128))
        lhs[f, COLS : COLS + EXTRA, :] = jnp.broadcast_to(weights, (EXTRA, rows)).astype(jnp.bfloat16)
        part = pl.ds(f * COLS, COLS)
        stat[0:8, part] = pmean[part, :].T[0:8, :]
        stat[8:16, part] = jnp.broadcast_to(count, (8, COLS))
        pmean[part, :] = pmean[part, :] / count

    for f in range(PHASES):
        for p in range(PIECES):
            near_copy(f, p).start()
    for f in range(PHASES):
        for p in range(PIECES):
            near_copy(f, p).wait_recv()
            half[f * PIECES + p] = turned[place(f, p, core), :] + near[f * PIECES + p]
            for d in range(1, yn):
                far_copy(f, p, d).start()
    panel_back(0)
    panel_weigh(0)

    def stat_copy(d):
        return remote(stat, stat_all.at[user], stat_s.at[d - 1], stat_r.at[d - 1],
                      lax.rem(user + d, users), item)

    def sum_copy(d):
        peer = lax.rem(user + d, users)
        return remote(sums.at[peer], sums_all.at[user], sum_s.at[d - 1], sum_r.at[d - 1], peer, item)

    def mean_copy(d):
        return remote(mean_mine, mean_all.at[item], mean_s.at[d - 1], mean_r.at[d - 1],
                      user, lax.rem(item + d, items))

    def x_copy(n, d):
        return remote(xsend.at[n, d - 1], xrecv.at[n, d - 1], xs.at[n, d - 1], xr.at[n, d - 1],
                      z * xn + lax.rem(x + d, xn), item)

    def z_copy(n, d):
        return remote(zsend.at[n, d - 1], zrecv.at[n, d - 1], zs.at[n, d - 1], zr.at[n, d - 1],
                      lax.rem(z + d, zn) * xn + x, item)

    def item_copy(n, d):
        peer = lax.rem(item + d, items)
        f, c = lax.div(n, cyc), lax.rem(n, cyc)
        return remote(icov.at[n, pl.ds(pl.multiple_of(peer * BLK, BLK), BLK)],
                      cov_ref.at[item * cyc + c, :, pl.ds(pl.multiple_of(f * COLS, COLS), COLS)],
                      is_.at[n, d - 1], ir.at[n, d - 1], user, peer)

    def compute(n):
        f, c = lax.div(n, cyc), lax.rem(n, cyc)

        @pl.when(f == 0)
        def _():
            load(c).wait()

        mean = pmean[pl.ds(pl.multiple_of(f * COLS, COLS), COLS), 0:1]

        wide = min(chunk, DOT)

        def tile(t, _):
            part = pl.ds(pl.multiple_of(t * wide, wide), wide)
            value = jnp.dot(lhs[f], xbuf[c, :, part], preferred_element_type=f32)
            total = value[COLS : COLS + 1, :]
            gram[:, part] = value[0:COLS, :] - mean * total

            @pl.when(f == 0)
            def _():
                for b in range(wide // width):
                    sums[t * (wide // width) + b, pl.ds(c, 1), :] = total[:, b * width : (b + 1) * width]

            return 0

        if chunk == wide:
            tile(0, 0)
        else:
            lax.fori_loop(0, chunk // wide, tile, 0)
        row = lax.broadcasted_iota(jnp.int32, (EXTRA, width), 0)
        for d in range(1, xn):
            scales = jnp.zeros((EXTRA, width), f32)
            for k in range(zn):
                start = pl.multiple_of((k * xn + lax.rem(x + d, xn)) * width, width)
                codes, code = encode(gram[:, pl.ds(start, width)])
                xsend[n, d - 1, k * COLS : (k + 1) * COLS, :] = codes
                scales = jnp.where(row == k, code, scales)
            xsend[n, d - 1, zn * COLS : zn * COLS + EXTRA, :] = scales.astype(jnp.int32).astype(jnp.int16)
            x_copy(n, d).start()
        for k in range(zn):
            start = pl.multiple_of((k * xn + x) * width, width)
            own[n, k] = gram[:, pl.ds(start, width)]

    def relay(n):
        for d in range(1, xn):
            x_copy(n, d).wait_recv()
            scales = xrecv[n, d - 1, zn * COLS : zn * COLS + EXTRA, :].astype(jnp.int32).astype(f32)
            for k in range(zn):
                codes = xrecv[n, d - 1, k * COLS : (k + 1) * COLS, :]
                own[n, k] = own[n, k] + decode(codes, scales[k : k + 1])
        for d in range(1, zn):
            codes, code = encode(own[n, lax.rem(z + d, zn)])
            zsend[n, d - 1, 0:COLS, :] = codes
            code = jnp.broadcast_to(code, (EXTRA, width))
            zsend[n, d - 1, COLS : COLS + EXTRA, :] = code.astype(jnp.int32).astype(jnp.int16)
            z_copy(n, d).start()

    def statistics():
        sums_all[user] = sums[user]
        stat_all[user] = stat[...]
        for d in range(1, users):
            stat_copy(d).wait_recv()
        whole = stat_all[0]
        for g in range(1, users):
            whole = whole + stat_all[g]
        panel_mean = whole[0:1, :] / whole[8:9, :]
        for g in range(users):
            delta = stat_all[g, 0:1, :] / stat_all[g, 8:9, :] - panel_mean
            shift[g] = jnp.broadcast_to(delta, (width, P_SIZE)).T
        for d in range(1, users):
            sum_copy(d).wait_recv()
        means = sums_all[0]
        for g in range(1, users):
            means = means + sums_all[g]
        mean_mine[...] = means / whole[8:9, 0:1]
        for d in range(1, items):
            mean_copy(d).start()
        mean_all[item] = mean_mine[...]

    def finish(n):
        f, c = lax.div(n, cyc), lax.rem(n, cyc)
        value = own[n, z]
        for g in range(users):
            part = pl.ds(pl.multiple_of(f * COLS, COLS), COLS)
            value = value + shift[g, part, :] * sums_all[g, pl.ds(c, 1), :]
        for d in range(1, zn):
            z_copy(n, d).wait_recv()
            code = zrecv[n, d - 1, COLS : COLS + EXTRA, :].astype(jnp.int32).astype(f32)[0:1]
            value = value + decode(zrecv[n, d - 1, 0:COLS, :], code)
        total = stat_all[0, 8:9, 0:1]
        for g in range(1, users):
            total = total + stat_all[g, 8:9, 0:1]
        icov[n] = (value / total).T
        for d in range(1, items):
            item_copy(n, d).start()
        part = pl.ds(pl.multiple_of(f * COLS, COLS), COLS)
        cov_ref[item * cyc + c, :, part] = icov[n, pl.ds(pl.multiple_of(item * BLK, BLK), BLK), :]

    lag = min(LAG, units)
    last = cyc + lag

    def step(s, _):
        @pl.when(s < units)
        def _():
            compute(s)

        @pl.when(s == min(1, cyc - 1))
        def _():
            for f in range(1, PHASES):
                panel_back(f)

        @pl.when(s == min(3, cyc - 1))
        def _():
            for f in range(1, PHASES):
                panel_weigh(f)
            for d in range(1, users):
                stat_copy(d).start()

        @pl.when(s == cyc - 1)
        def _():
            for d in range(1, users):
                sum_copy(d).start()

        @pl.when(s >= lag)
        def _():
            relay(s - lag)

        @pl.when(s == last)
        def _():
            statistics()

        @pl.when(s >= last)
        def _():
            for k in range(PHASES):
                finish((s - last) * PHASES + k)

        return 0

    lax.fori_loop(0, units + lag, step, 0)

    for d in range(1, items):
        mean_copy(d).wait()
    for i in range(items):
        value = jnp.zeros((mean_all.shape[1], BLK), f32)
        for k in range(items):
            value = jnp.where(item == k, mean_all[i, :, k * BLK : (k + 1) * BLK], value)
        mean_ref[i * cyc : (i + 1) * cyc, :] = value[0:cyc]

    for f in range(PHASES):
        for p in range(PIECES):
            near_copy(f, p).wait_send()
            back_copy(f, p).wait_send()
            for d in range(1, yn):
                far_copy(f, p, d).wait_send()
    for d in range(1, users):
        stat_copy(d).wait_send()
        sum_copy(d).wait_send()

    def drain(n, _):
        for d in range(1, xn):
            x_copy(n, d).wait_send()
        for d in range(1, zn):
            z_copy(n, d).wait_send()
        for d in range(1, items):
            item_copy(n, d).wait()
        return 0

    lax.fori_loop(0, units, drain, 0)


def hand_over_kernel(cov_ref, mean_ref, cov_out, mean_out, sem):
    whole = pltpu.make_async_copy(cov_ref, cov_out, sem.at[0])
    means = pltpu.make_async_copy(mean_ref, mean_out, sem.at[1])
    whole.start()
    means.start()
    whole.wait()
    means.wait()


def hand_over(cov, mean):
    anywhere = pl.BlockSpec(memory_space=pl.ANY)
    vmem = pl.BlockSpec(memory_space=pltpu.VMEM)
    return pl.pallas_call(
        hand_over_kernel,
        out_shape=(
            jax.ShapeDtypeStruct(cov.shape, f32), jax.ShapeDtypeStruct(mean.shape, f32),
        ),
        in_specs=[vmem, vmem],
        out_specs=(anywhere, anywhere),
        scratch_shapes=[pltpu.SemaphoreType.DMA((2,))],
        name="hand_over",
    )(cov, mean)


def per_device(interactions, user_weights, panel_index):
    rows, shard = interactions.shape
    users, items = lax.axis_size("users"), lax.axis_size("items")
    zn = 4 if users % 4 == 0 else 1
    xn = users // zn
    width = items * BLK
    cyc = shard // (users * width)
    cyc8 = -(-cyc // 8) * 8
    yn = items // 2
    per_shard = shard // P_SIZE
    chosen = panel_index[0]
    local = lax.dynamic_slice_in_dim(interactions, chosen % per_shard * P_SIZE, P_SIZE, 1)
    local = jnp.where(lax.axis_index("items") == chosen // per_shard, local, jnp.zeros_like(local))
    weights = user_weights.reshape(rows // 128, 128)

    bf16, i16 = jnp.bfloat16, jnp.int16
    piece, tall = COLS // 2 // PIECES, COLS + EXTRA
    pieces, units = PHASES * PIECES, PHASES * cyc
    dma = pltpu.SemaphoreType.DMA
    vmem = pl.BlockSpec(memory_space=pltpu.VMEM)
    cov, mean = pl.pallas_call(
        functools.partial(kernel, (users, items, xn, zn, cyc, width)),
        out_shape=(
            jax.ShapeDtypeStruct((items * cyc, BLK, P_SIZE), f32),
            jax.ShapeDtypeStruct((items * cyc, BLK), f32),
        ),
        in_specs=[pl.BlockSpec(memory_space=pl.ANY), vmem, vmem],
        out_specs=(vmem, vmem),
        scratch_shapes=[
            pltpu.VMEM((cyc, rows, users * width), bf16),
            pltpu.VMEM((P_SIZE, rows), bf16),
            pltpu.VMEM((P_SIZE, rows), bf16),
            pltpu.VMEM((pieces, piece, rows), bf16),
            pltpu.VMEM((pieces, piece, rows), bf16),
            pltpu.VMEM((pieces, yn - 1, piece, rows), bf16),
            pltpu.VMEM((PHASES, tall, rows), bf16),
            pltpu.VMEM((P_SIZE, 128), f32),
            pltpu.VMEM((COLS, users * width), f32),
            pltpu.VMEM((units, zn, COLS, width), f32),
            pltpu.VMEM((units, xn - 1, zn * COLS + EXTRA, width), i16),
            pltpu.VMEM((units, xn - 1, zn * COLS + EXTRA, width), i16),
            pltpu.VMEM((units, zn - 1, tall, width), i16),
            pltpu.VMEM((units, zn - 1, tall, width), i16),
            pltpu.VMEM((units, width, COLS), f32),
            pltpu.VMEM((users, cyc8, width), f32),
            pltpu.VMEM((users, cyc8, width), f32),
            pltpu.VMEM((16, P_SIZE), f32),
            pltpu.VMEM((users, 16, P_SIZE), f32),
            pltpu.VMEM((users, P_SIZE, width), f32),
            pltpu.VMEM((cyc8, width), f32),
            pltpu.VMEM((items, cyc8, width), f32),
            dma((cyc,)),
            dma((pieces,)), dma((pieces,)),
            dma((pieces, yn - 1)), dma((pieces, yn - 1)),
            dma((pieces,)), dma((pieces,)),
            dma((units, xn - 1)), dma((units, xn - 1)),
            dma((units, zn - 1)), dma((units, zn - 1)),
            dma((units, items - 1)), dma((units, items - 1)),
            dma((users - 1,)), dma((users - 1,)),
            dma((users - 1,)), dma((users - 1,)),
            dma((items - 1,)), dma((items - 1,)),
        ],
        compiler_params=pltpu.CompilerParams(
            collective_id=0, has_side_effects=True, vmem_limit_bytes=60 * 2**20
        ),
        cost_estimate=pl.CostEstimate(
            flops=2 * P_SIZE * rows * shard, bytes_accessed=2 * rows * shard, transcendentals=0
        ),
        name="panel_covariance",
    )(interactions, local, weights)
    return hand_over(cov, mean)


def solution(mesh):
    return jax.shard_map(
        per_device,
        mesh=mesh,
        in_specs=(P("users", "items"), P("users"), P()),
        out_specs=(P(None, ("users", "items"), None), P(None, ("users", "items"))),
        check_vma=False,
    )
```

```python
import functools
import math

import jax
import jax.numpy as jnp
from jax import lax
from jax.experimental import pallas as pl
from jax.experimental.pallas import tpu as pltpu
from jax.sharding import PartitionSpec as P

P_SIZE = 256
BLK = 32
EXTRA = 16
TILE = 256
DOT = 1024
PHASES = 2
COLS = P_SIZE // PHASES
PIECES = 2
LAG = 2
STEP = math.log(2.0) / 256.0
TOP = 32600.0
f32 = jnp.float32


def encode(block):
    top = jnp.max(jnp.abs(block), axis=0, keepdims=True)
    code = jnp.ceil(jnp.log(jnp.maximum(top, 1e-30)) * (1.0 / STEP)) + 1.0
    scaled = jnp.round(block * (jnp.exp(code * -STEP) * TOP))
    return scaled.astype(jnp.int32).astype(jnp.int16), code


def decode(codes, code):
    return codes.astype(jnp.int32).astype(f32) * (jnp.exp(code * STEP) * (1.0 / TOP))


def kernel(
    sizes, x_ref, loc_ref, w_ref, cov_ref, mean_ref,
    xbuf, turned, full, half, near, far, lhs, pmean, gram, own,
    xsend, xrecv, zsend, zrecv, icov, sums, sums_all, stat, stat_all, shift, mean_mine, mean_all,
    load_sem, near_s, near_r, far_s, far_r, back_s, back_r, xs, xr, zs, zr, is_, ir,
    sum_s, sum_r, stat_s, stat_r, mean_s, mean_r,
):
    users, items, xn, zn, cyc, width = sizes
    rows = loc_ref.shape[0]
    chunk = users * width
    user, item = lax.axis_index("users"), lax.axis_index("items")
    z, x = lax.div(user, xn), lax.rem(user, xn)
    y, core = lax.div(item, 2), lax.rem(item, 2)
    yn = items // 2
    units = PHASES * cyc

    def load(c):
        return pltpu.make_async_copy(x_ref.at[:, pl.ds(c * chunk, chunk)], xbuf.at[c], load_sem.at[c])

    def remote(src, dst, send, recv, to_user, to_item):
        return pltpu.make_async_remote_copy(
            src_ref=src, dst_ref=dst, send_sem=send, recv_sem=recv,
            device_id={"users": to_user, "items": to_item},
            device_id_type=pl.DeviceIdType.MESH,
        )

    for c in range(cyc):
        load(c).start()

    barrier = pltpu.get_barrier_semaphore()
    for d in range(1, users):
        pl.semaphore_signal(
            barrier, inc=1, device_id={"users": lax.rem(user + d, users), "items": item},
            device_id_type=pl.DeviceIdType.MESH,
        )
    for d in range(1, items):
        pl.semaphore_signal(
            barrier, inc=1, device_id={"users": user, "items": lax.rem(item + d, items)},
            device_id_type=pl.DeviceIdType.MESH,
        )
    for r in range(rows // TILE):
        part = pl.ds(r * TILE, TILE)
        turned[:, part] = loc_ref[part, :].astype(f32).T.astype(jnp.bfloat16)
    pl.semaphore_wait(barrier, users + items - 2)

    side = COLS // 2
    piece = side // PIECES

    def place(f, p, whose):
        return pl.ds(pl.multiple_of(f * COLS + whose * side + p * piece, piece), piece)

    def near_copy(f, p):
        n = f * PIECES + p
        return remote(turned.at[place(f, p, 1 - core)], near.at[n],
                      near_s.at[n], near_r.at[n], user, y * 2 + 1 - core)

    def far_copy(f, p, d):
        n = f * PIECES + p
        return remote(half.at[n], far.at[n, d - 1], far_s.at[n, d - 1], far_r.at[n, d - 1],
                      user, lax.rem(y + d, yn) * 2 + core)

    def back_copy(f, p):
        n = f * PIECES + p
        return remote(full.at[place(f, p, core)], full.at[place(f, p, core)],
                      back_s.at[n], back_r.at[n], user, y * 2 + 1 - core)

    def panel_back(f):
        for p in range(PIECES):
            value = half[f * PIECES + p]
            for d in range(1, yn):
                far_copy(f, p, d).wait_recv()
                value = value + far[f * PIECES + p, d - 1]
            full[place(f, p, core), :] = value
            back_copy(f, p).start()

    def panel_weigh(f):
        for p in range(PIECES):
            back_copy(f, p).wait_recv()
        weights = jnp.concatenate([w_ref[r : r + 1, :] for r in range(rows // 128)], axis=1).astype(f32)
        count = jnp.sum(weights, axis=1, keepdims=True)
        for r in range(0, COLS, 64):
            part = pl.ds(f * COLS + r, 64)
            product = full[part, :].astype(f32) * weights
            lhs[f, r : r + 64, :] = product.astype(jnp.bfloat16)
            pmean[part, :] = jnp.broadcast_to(jnp.sum(product, axis=1, keepdims=True), (64, 128))
        lhs[f, COLS : COLS + EXTRA, :] = jnp.broadcast_to(weights, (EXTRA, rows)).astype(jnp.bfloat16)
        part = pl.ds(f * COLS, COLS)
        stat[0:8, part] = pmean[part, :].T[0:8, :]
        stat[8:16, part] = jnp.broadcast_to(count, (8, COLS))
        pmean[part, :] = pmean[part, :] / count

    for f in range(PHASES):
        for p in range(PIECES):
            near_copy(f, p).start()
    for f in range(PHASES):
        for p in range(PIECES):
            near_copy(f, p).wait_recv()
            half[f * PIECES + p] = turned[place(f, p, core), :] + near[f * PIECES + p]
            for d in range(1, yn):
                far_copy(f, p, d).start()
    panel_back(0)
    panel_weigh(0)

    def stat_copy(d):
        return remote(stat, stat_all.at[user], stat_s.at[d - 1], stat_r.at[d - 1],
                      lax.rem(user + d, users), item)

    def sum_copy(d):
        peer = lax.rem(user + d, users)
        return remote(sums.at[peer], sums_all.at[user], sum_s.at[d - 1], sum_r.at[d - 1], peer, item)

    def mean_copy(d):
        return remote(mean_mine, mean_all.at[item], mean_s.at[d - 1], mean_r.at[d - 1],
                      user, lax.rem(item + d, items))

    def x_copy(n, d):
        return remote(xsend.at[n, d - 1], xrecv.at[n, d - 1], xs.at[n, d - 1], xr.at[n, d - 1],
                      z * xn + lax.rem(x + d, xn), item)

    def z_copy(n, block, slot, to):
        return remote(zsend.at[n, block], zrecv.at[n, slot], zs.at[n, block], zr.at[n, slot],
                      to * xn + x, item)

    def z_arrived(n, slot):
        z_copy(n, 0, slot, lax.rem(z + 1, zn)).wait_recv()
        code = zrecv[n, slot, COLS : COLS + EXTRA, :].astype(jnp.int32).astype(f32)[0:1]
        return decode(zrecv[n, slot, 0:COLS, :], code)

    def item_copy(n, d):
        peer = lax.rem(item + d, items)
        f, c = lax.div(n, cyc), lax.rem(n, cyc)
        return remote(icov.at[n, pl.ds(pl.multiple_of(peer * BLK, BLK), BLK)],
                      cov_ref.at[item * cyc + c, :, pl.ds(pl.multiple_of(f * COLS, COLS), COLS)],
                      is_.at[n, d - 1], ir.at[n, d - 1], user, peer)

    def compute(n):
        f, c = lax.div(n, cyc), lax.rem(n, cyc)

        @pl.when(f == 0)
        def _():
            load(c).wait()

        mean = pmean[pl.ds(pl.multiple_of(f * COLS, COLS), COLS), 0:1]

        wide = min(chunk, DOT)

        def tile(t, _):
            part = pl.ds(pl.multiple_of(t * wide, wide), wide)
            value = jnp.dot(lhs[f], xbuf[c, :, part], preferred_element_type=f32)
            total = value[COLS : COLS + 1, :]
            gram[:, part] = value[0:COLS, :] - mean * total

            @pl.when(f == 0)
            def _():
                for b in range(wide // width):
                    sums[t * (wide // width) + b, pl.ds(c, 1), :] = total[:, b * width : (b + 1) * width]

            return 0

        if chunk == wide:
            tile(0, 0)
        else:
            lax.fori_loop(0, chunk // wide, tile, 0)
        row = lax.broadcasted_iota(jnp.int32, (EXTRA, width), 0)
        for d in range(1, xn):
            scales = jnp.zeros((EXTRA, width), f32)
            for k in range(zn):
                start = pl.multiple_of((k * xn + lax.rem(x + d, xn)) * width, width)
                codes, code = encode(gram[:, pl.ds(start, width)])
                xsend[n, d - 1, k * COLS : (k + 1) * COLS, :] = codes
                scales = jnp.where(row == k, code, scales)
            xsend[n, d - 1, zn * COLS : zn * COLS + EXTRA, :] = scales.astype(jnp.int32).astype(jnp.int16)
            x_copy(n, d).start()
        for k in range(zn):
            start = pl.multiple_of((k * xn + x) * width, width)
            own[n, k] = gram[:, pl.ds(start, width)]

    def relay(n):
        for d in range(1, xn):
            x_copy(n, d).wait_recv()
            scales = xrecv[n, d - 1, zn * COLS : zn * COLS + EXTRA, :].astype(jnp.int32).astype(f32)
            for k in range(zn):
                codes = xrecv[n, d - 1, k * COLS : (k + 1) * COLS, :]
                own[n, k] = own[n, k] + decode(codes, scales[k : k + 1])

    def z_send(n, at, block, step_z):
        value = own[n, block]
        if 0 <= at - step_z < zn:
            value = value + z_arrived(n, block)
        codes, code = encode(value)
        zsend[n, block, 0:COLS, :] = codes
        code = jnp.broadcast_to(code, (EXTRA, width))
        zsend[n, block, COLS : COLS + EXTRA, :] = code.astype(jnp.int32).astype(jnp.int16)
        slot = zn if step_z < 0 and block == at - 1 else block
        z_copy(n, block, slot, at + step_z).start()

    def hop(n, h):
        @pl.when(z == h)
        def _():
            for block in range(h + 1, zn):
                z_send(n, h, block, 1)

        @pl.when(z == zn - 1 - h)
        def _():
            for block in range(0, zn - 1 - h):
                z_send(n, zn - 1 - h, block, -1)

    def statistics():
        sums_all[user] = sums[user]
        stat_all[user] = stat[...]
        for d in range(1, users):
            stat_copy(d).wait_recv()
        whole = stat_all[0]
        for g in range(1, users):
            whole = whole + stat_all[g]
        panel_mean = whole[0:1, :] / whole[8:9, :]
        for g in range(users):
            delta = stat_all[g, 0:1, :] / stat_all[g, 8:9, :] - panel_mean
            shift[g] = jnp.broadcast_to(delta, (width, P_SIZE)).T
        for d in range(1, users):
            sum_copy(d).wait_recv()
        means = sums_all[0]
        for g in range(1, users):
            means = means + sums_all[g]
        mean_mine[...] = means / whole[8:9, 0:1]
        for d in range(1, items):
            mean_copy(d).start()
        mean_all[item] = mean_mine[...]

    def finish(n):
        f, c = lax.div(n, cyc), lax.rem(n, cyc)
        for k in range(zn):
            @pl.when(z == k)
            def _():
                value = own[n, k]
                if k > 0:
                    value = value + z_arrived(n, k)
                if k < zn - 1:
                    value = value + z_arrived(n, zn)
                own[n, k] = value

        value = own[n, z]
        for g in range(users):
            part = pl.ds(pl.multiple_of(f * COLS, COLS), COLS)
            value = value + shift[g, part, :] * sums_all[g, pl.ds(c, 1), :]
        total = stat_all[0, 8:9, 0:1]
        for g in range(1, users):
            total = total + stat_all[g, 8:9, 0:1]
        icov[n] = (value / total).T
        for d in range(1, items):
            item_copy(n, d).start()
        part = pl.ds(pl.multiple_of(f * COLS, COLS), COLS)
        cov_ref[item * cyc + c, :, part] = icov[n, pl.ds(pl.multiple_of(item * BLK, BLK), BLK), :]

    lag = min(LAG, units)
    hops = zn - 1
    last = cyc + lag + hops

    def step(s, _):
        @pl.when(s < units)
        def _():
            compute(s)

        @pl.when(s == min(1, cyc - 1))
        def _():
            for f in range(1, PHASES):
                panel_back(f)

        @pl.when(s == min(3, cyc - 1))
        def _():
            for f in range(1, PHASES):
                panel_weigh(f)
            for d in range(1, users):
                stat_copy(d).start()

        @pl.when(s == cyc - 1)
        def _():
            for d in range(1, users):
                sum_copy(d).start()

        @pl.when(s >= lag)
        def _():
            @pl.when(s < units + lag)
            def _():
                relay(s - lag)

        for h in range(hops):
            @pl.when((s >= lag + h) & (s < units + lag + h))
            def _():
                hop(s - lag - h, h)

        @pl.when(s == last)
        def _():
            statistics()

        @pl.when(s >= last)
        def _():
            for k in range(PHASES):
                finish((s - last) * PHASES + k)

        return 0

    lax.fori_loop(0, units + lag + hops, step, 0)

    for d in range(1, items):
        mean_copy(d).wait()
    for i in range(items):
        value = jnp.zeros((mean_all.shape[1], BLK), f32)
        for k in range(items):
            value = jnp.where(item == k, mean_all[i, :, k * BLK : (k + 1) * BLK], value)
        mean_ref[i * cyc : (i + 1) * cyc, :] = value[0:cyc]

    for f in range(PHASES):
        for p in range(PIECES):
            near_copy(f, p).wait_send()
            back_copy(f, p).wait_send()
            for d in range(1, yn):
                far_copy(f, p, d).wait_send()
    for d in range(1, users):
        stat_copy(d).wait_send()
        sum_copy(d).wait_send()

    def drain(n, _):
        for d in range(1, xn):
            x_copy(n, d).wait_send()
        for k in range(zn):
            @pl.when(z != k)
            def _():
                z_copy(n, k, k, lax.rem(z + 1, zn)).wait_send()
        for d in range(1, items):
            item_copy(n, d).wait()
        return 0

    lax.fori_loop(0, units, drain, 0)


def hand_over_kernel(cov_ref, mean_ref, cov_out, mean_out, sem):
    whole = pltpu.make_async_copy(cov_ref, cov_out, sem.at[0])
    means = pltpu.make_async_copy(mean_ref, mean_out, sem.at[1])
    whole.start()
    means.start()
    whole.wait()
    means.wait()


def hand_over(cov, mean):
    anywhere = pl.BlockSpec(memory_space=pl.ANY)
    vmem = pl.BlockSpec(memory_space=pltpu.VMEM)
    return pl.pallas_call(
        hand_over_kernel,
        out_shape=(
            jax.ShapeDtypeStruct(cov.shape, f32), jax.ShapeDtypeStruct(mean.shape, f32),
        ),
        in_specs=[vmem, vmem],
        out_specs=(anywhere, anywhere),
        scratch_shapes=[pltpu.SemaphoreType.DMA((2,))],
        name="hand_over",
    )(cov, mean)


def per_device(interactions, user_weights, panel_index):
    rows, shard = interactions.shape
    users, items = lax.axis_size("users"), lax.axis_size("items")
    zn = 4 if users % 4 == 0 else 1
    xn = users // zn
    width = items * BLK
    cyc = shard // (users * width)
    cyc8 = -(-cyc // 8) * 8
    yn = items // 2
    per_shard = shard // P_SIZE
    chosen = panel_index[0]
    local = lax.dynamic_slice_in_dim(interactions, chosen % per_shard * P_SIZE, P_SIZE, 1)
    local = jnp.where(lax.axis_index("items") == chosen // per_shard, local, jnp.zeros_like(local))
    weights = user_weights.reshape(rows // 128, 128)

    bf16, i16 = jnp.bfloat16, jnp.int16
    piece, tall = COLS // 2 // PIECES, COLS + EXTRA
    pieces, units = PHASES * PIECES, PHASES * cyc
    dma = pltpu.SemaphoreType.DMA
    vmem = pl.BlockSpec(memory_space=pltpu.VMEM)
    cov, mean = pl.pallas_call(
        functools.partial(kernel, (users, items, xn, zn, cyc, width)),
        out_shape=(
            jax.ShapeDtypeStruct((items * cyc, BLK, P_SIZE), f32),
            jax.ShapeDtypeStruct((items * cyc, BLK), f32),
        ),
        in_specs=[pl.BlockSpec(memory_space=pl.ANY), vmem, vmem],
        out_specs=(vmem, vmem),
        scratch_shapes=[
            pltpu.VMEM((cyc, rows, users * width), bf16),
            pltpu.VMEM((P_SIZE, rows), bf16),
            pltpu.VMEM((P_SIZE, rows), bf16),
            pltpu.VMEM((pieces, piece, rows), bf16),
            pltpu.VMEM((pieces, piece, rows), bf16),
            pltpu.VMEM((pieces, yn - 1, piece, rows), bf16),
            pltpu.VMEM((PHASES, tall, rows), bf16),
            pltpu.VMEM((P_SIZE, 128), f32),
            pltpu.VMEM((COLS, users * width), f32),
            pltpu.VMEM((units, zn, COLS, width), f32),
            pltpu.VMEM((units, xn - 1, zn * COLS + EXTRA, width), i16),
            pltpu.VMEM((units, xn - 1, zn * COLS + EXTRA, width), i16),
            pltpu.VMEM((units, zn, tall, width), i16),
            pltpu.VMEM((units, zn + 1, tall, width), i16),
            pltpu.VMEM((units, width, COLS), f32),
            pltpu.VMEM((users, cyc8, width), f32),
            pltpu.VMEM((users, cyc8, width), f32),
            pltpu.VMEM((16, P_SIZE), f32),
            pltpu.VMEM((users, 16, P_SIZE), f32),
            pltpu.VMEM((users, P_SIZE, width), f32),
            pltpu.VMEM((cyc8, width), f32),
            pltpu.VMEM((items, cyc8, width), f32),
            dma((cyc,)),
            dma((pieces,)), dma((pieces,)),
            dma((pieces, yn - 1)), dma((pieces, yn - 1)),
            dma((pieces,)), dma((pieces,)),
            dma((units, xn - 1)), dma((units, xn - 1)),
            dma((units, zn)), dma((units, zn + 1)),
            dma((units, items - 1)), dma((units, items - 1)),
            dma((users - 1,)), dma((users - 1,)),
            dma((users - 1,)), dma((users - 1,)),
            dma((items - 1,)), dma((items - 1,)),
        ],
        compiler_params=pltpu.CompilerParams(
            collective_id=0, has_side_effects=True, vmem_limit_bytes=60 * 2**20
        ),
        cost_estimate=pl.CostEstimate(
            flops=2 * P_SIZE * rows * shard, bytes_accessed=2 * rows * shard, transcendentals=0
        ),
        name="panel_covariance",
    )(interactions, local, weights)
    return hand_over(cov, mean)


def solution(mesh):
    return jax.shard_map(
        per_device,
        mesh=mesh,
        in_specs=(P("users", "items"), P("users"), P()),
        out_specs=(P(None, ("users", "items"), None), P(None, ("users", "items"))),
        check_vma=False,
    )
```

```python
import functools
import math

import jax
import jax.numpy as jnp
from jax import lax
from jax.experimental import pallas as pl
from jax.experimental.pallas import tpu as pltpu
from jax.sharding import PartitionSpec as P

P_SIZE = 256
BLK = 32
EXTRA = 16
TILE = 256
DOT = 1024
PHASES = 2
COLS = P_SIZE // PHASES
PIECES = 2
LAG = 2
EVERY, FIRST = 8, 2
STEP = math.log(2.0) / 256.0
TOP = 32600.0
f32 = jnp.float32


def encode(block):
    top = jnp.max(jnp.abs(block), axis=0, keepdims=True)
    code = jnp.ceil(jnp.log(jnp.maximum(top, 1e-30)) * (1.0 / STEP)) + 1.0
    scaled = jnp.round(block * (jnp.exp(code * -STEP) * TOP))
    return scaled.astype(jnp.int32).astype(jnp.int16), code


def decode(codes, code):
    return codes.astype(jnp.int32).astype(f32) * (jnp.exp(code * STEP) * (1.0 / TOP))


def kernel(
    sizes, x_ref, loc_ref, w_ref, cov_ref, mean_ref,
    xbuf, turned, full, half, near, far, lhs, pmean, gram, own,
    xsend, xrecv, late_send, late_recv, zsend, zrecv, icov, sums, sums_all, stat, stat_all, shift, mean_mine, mean_all,
    load_sem, near_s, near_r, far_s, far_r, back_s, back_r, xs, xr, ls, lr, zs, zr, is_, ir,
    sum_s, sum_r, stat_s, stat_r, mean_s, mean_r,
):
    users, items, xn, zn, cyc, width = sizes
    rows = loc_ref.shape[0]
    chunk = users * width
    user, item = lax.axis_index("users"), lax.axis_index("items")
    z, x = lax.div(user, xn), lax.rem(user, xn)
    y, core = lax.div(item, 2), lax.rem(item, 2)
    yn = items // 2
    units = PHASES * cyc

    def load(c):
        return pltpu.make_async_copy(x_ref.at[:, pl.ds(c * chunk, chunk)], xbuf.at[c], load_sem.at[c])

    def remote(src, dst, send, recv, to_user, to_item):
        return pltpu.make_async_remote_copy(
            src_ref=src, dst_ref=dst, send_sem=send, recv_sem=recv,
            device_id={"users": to_user, "items": to_item},
            device_id_type=pl.DeviceIdType.MESH,
        )

    for c in range(cyc):
        load(c).start()

    barrier = pltpu.get_barrier_semaphore()
    for d in range(1, users):
        pl.semaphore_signal(
            barrier, inc=1, device_id={"users": lax.rem(user + d, users), "items": item},
            device_id_type=pl.DeviceIdType.MESH,
        )
    for d in range(1, items):
        pl.semaphore_signal(
            barrier, inc=1, device_id={"users": user, "items": lax.rem(item + d, items)},
            device_id_type=pl.DeviceIdType.MESH,
        )
    for r in range(rows // TILE):
        part = pl.ds(r * TILE, TILE)
        turned[:, part] = loc_ref[part, :].astype(f32).T.astype(jnp.bfloat16)
    pl.semaphore_wait(barrier, users + items - 2)

    side = COLS // 2
    piece = side // PIECES

    def place(f, p, whose):
        return pl.ds(pl.multiple_of(f * COLS + whose * side + p * piece, piece), piece)

    def near_copy(f, p):
        n = f * PIECES + p
        return remote(turned.at[place(f, p, 1 - core)], near.at[n],
                      near_s.at[n], near_r.at[n], user, y * 2 + 1 - core)

    def far_copy(f, p, d):
        n = f * PIECES + p
        return remote(half.at[n], far.at[n, d - 1], far_s.at[n, d - 1], far_r.at[n, d - 1],
                      user, lax.rem(y + d, yn) * 2 + core)

    def back_copy(f, p):
        n = f * PIECES + p
        return remote(full.at[place(f, p, core)], full.at[place(f, p, core)],
                      back_s.at[n], back_r.at[n], user, y * 2 + 1 - core)

    def panel_back(f):
        for p in range(PIECES):
            value = half[f * PIECES + p]
            for d in range(1, yn):
                far_copy(f, p, d).wait_recv()
                value = value + far[f * PIECES + p, d - 1]
            full[place(f, p, core), :] = value
            back_copy(f, p).start()

    def panel_weigh(f):
        for p in range(PIECES):
            back_copy(f, p).wait_recv()
        weights = jnp.concatenate([w_ref[r : r + 1, :] for r in range(rows // 128)], axis=1).astype(f32)
        count = jnp.sum(weights, axis=1, keepdims=True)
        for r in range(0, COLS, 64):
            part = pl.ds(f * COLS + r, 64)
            product = full[part, :].astype(f32) * weights
            lhs[f, r : r + 64, :] = product.astype(jnp.bfloat16)
            pmean[part, :] = jnp.broadcast_to(jnp.sum(product, axis=1, keepdims=True), (64, 128))
        lhs[f, COLS : COLS + EXTRA, :] = jnp.broadcast_to(weights, (EXTRA, rows)).astype(jnp.bfloat16)
        part = pl.ds(f * COLS, COLS)
        stat[0:8, part] = pmean[part, :].T[0:8, :]
        stat[8:16, part] = jnp.broadcast_to(count, (8, COLS))
        pmean[part, :] = pmean[part, :] / count

    for f in range(PHASES):
        for p in range(PIECES):
            near_copy(f, p).start()
    for f in range(PHASES):
        for p in range(PIECES):
            near_copy(f, p).wait_recv()
            half[f * PIECES + p] = turned[place(f, p, core), :] + near[f * PIECES + p]
            for d in range(1, yn):
                far_copy(f, p, d).start()
    panel_back(0)
    panel_weigh(0)

    def stat_copy(d):
        return remote(stat, stat_all.at[user], stat_s.at[d - 1], stat_r.at[d - 1],
                      lax.rem(user + d, users), item)

    def sum_copy(d):
        peer = lax.rem(user + d, users)
        return remote(sums.at[peer], sums_all.at[user], sum_s.at[d - 1], sum_r.at[d - 1], peer, item)

    def mean_copy(d):
        return remote(mean_mine, mean_all.at[item], mean_s.at[d - 1], mean_r.at[d - 1],
                      user, lax.rem(item + d, items))

    def x_copy(n, d):
        return remote(xsend.at[n, d - 1], xrecv.at[n, d - 1], xs.at[n, d - 1], xr.at[n, d - 1],
                      z * xn + lax.rem(x + d, xn), item)

    def z_first(n):
        return lax.rem(n, EVERY) == FIRST

    def beside(n, d):
        return units + lax.div(n, EVERY) * (xn - 1) + d - 1

    def late_copy(n, d):
        i = lax.div(n, EVERY)
        return remote(late_send.at[i, d - 1], late_recv.at[i, d - 1], ls.at[i, d - 1], lr.at[i, d - 1],
                      z * xn + lax.rem(x + d, xn), item)

    def z_copy(n, block, slot, to):
        return remote(zsend.at[n, block], zrecv.at[n, slot], zs.at[n, block], zr.at[n, slot],
                      to * xn + x, item)

    def z_arrived(n, slot):
        z_copy(n, 0, slot, lax.rem(z + 1, zn)).wait_recv()
        code = zrecv[n, slot, COLS : COLS + EXTRA, :].astype(jnp.int32).astype(f32)[0:1]
        return decode(zrecv[n, slot, 0:COLS, :], code)

    def item_copy(n, d):
        peer = lax.rem(item + d, items)
        f, c = lax.div(n, cyc), lax.rem(n, cyc)
        return remote(icov.at[n, pl.ds(pl.multiple_of(peer * BLK, BLK), BLK)],
                      cov_ref.at[item * cyc + c, :, pl.ds(pl.multiple_of(f * COLS, COLS), COLS)],
                      is_.at[n, d - 1], ir.at[n, d - 1], user, peer)

    def compute(n):
        f, c = lax.div(n, cyc), lax.rem(n, cyc)

        @pl.when(f == 0)
        def _():
            load(c).wait()

        mean = pmean[pl.ds(pl.multiple_of(f * COLS, COLS), COLS), 0:1]

        wide = min(chunk, DOT)

        def tile(t, _):
            part = pl.ds(pl.multiple_of(t * wide, wide), wide)
            value = jnp.dot(lhs[f], xbuf[c, :, part], preferred_element_type=f32)
            total = value[COLS : COLS + 1, :]
            gram[:, part] = value[0:COLS, :] - mean * total

            @pl.when(f == 0)
            def _():
                for b in range(wide // width):
                    sums[t * (wide // width) + b, pl.ds(c, 1), :] = total[:, b * width : (b + 1) * width]

            return 0

        if chunk == wide:
            tile(0, 0)
        else:
            lax.fori_loop(0, chunk // wide, tile, 0)
        @pl.when(z_first(n))
        def _():
            for d in range(1, xn):
                for k in range(zn):
                    start = pl.multiple_of((k * xn + lax.rem(x + d, xn)) * width, width)
                    own[beside(n, d), k] = gram[:, pl.ds(start, width)]

        @pl.when(jnp.logical_not(z_first(n)))
        def _():
            row = lax.broadcasted_iota(jnp.int32, (EXTRA, width), 0)
            for d in range(1, xn):
                scales = jnp.zeros((EXTRA, width), f32)
                for k in range(zn):
                    start = pl.multiple_of((k * xn + lax.rem(x + d, xn)) * width, width)
                    codes, code = encode(gram[:, pl.ds(start, width)])
                    xsend[n, d - 1, k * COLS : (k + 1) * COLS, :] = codes
                    scales = jnp.where(row == k, code, scales)
                scales = scales.astype(jnp.int32).astype(jnp.int16)
                xsend[n, d - 1, zn * COLS : zn * COLS + EXTRA, :] = scales
                x_copy(n, d).start()

        for k in range(zn):
            start = pl.multiple_of((k * xn + x) * width, width)
            own[n, k] = gram[:, pl.ds(start, width)]

    def relay(n):
        for d in range(1, xn):
            x_copy(n, d).wait_recv()
            scales = xrecv[n, d - 1, zn * COLS : zn * COLS + EXTRA, :].astype(jnp.int32).astype(f32)
            for k in range(zn):
                codes = xrecv[n, d - 1, k * COLS : (k + 1) * COLS, :]
                own[n, k] = own[n, k] + decode(codes, scales[k : k + 1])

    def z_send(n, at, block, step_z):
        value = own[n, block]
        if 0 <= at - step_z < zn:
            value = value + z_arrived(n, block)
        codes, code = encode(value)
        zsend[n, block, 0:COLS, :] = codes
        code = jnp.broadcast_to(code, (EXTRA, width))
        zsend[n, block, COLS : COLS + EXTRA, :] = code.astype(jnp.int32).astype(jnp.int16)
        slot = zn if step_z < 0 and block == at - 1 else block
        z_copy(n, block, slot, at + step_z).start()

    def hop(n, h):
        @pl.when(z == h)
        def _():
            for block in range(h + 1, zn):
                z_send(n, h, block, 1)

            @pl.when(z_first(n))
            def _():
                for d in range(1, xn):
                    for block in range(h + 1, zn):
                        z_send(beside(n, d), h, block, 1)

        @pl.when(z == zn - 1 - h)
        def _():
            for block in range(0, zn - 1 - h):
                z_send(n, zn - 1 - h, block, -1)

            @pl.when(z_first(n))
            def _():
                for d in range(1, xn):
                    for block in range(0, zn - 1 - h):
                        z_send(beside(n, d), zn - 1 - h, block, -1)

    def home(n):
        for k in range(zn):
            @pl.when(z == k)
            def _():
                value = own[n, k]
                if k > 0:
                    value = value + z_arrived(n, k)
                if k < zn - 1:
                    value = value + z_arrived(n, zn)
                own[n, k] = value

    def late(n):
        for d in range(1, xn):
            home(beside(n, d))
            codes, code = encode(own[beside(n, d), z])
            i = lax.div(n, EVERY)
            late_send[i, d - 1, 0:COLS, :] = codes
            code = jnp.broadcast_to(code, (EXTRA, width))
            late_send[i, d - 1, COLS : COLS + EXTRA, :] = code.astype(jnp.int32).astype(jnp.int16)
            late_copy(n, d).start()

    def statistics():
        sums_all[user] = sums[user]
        stat_all[user] = stat[...]
        for d in range(1, users):
            stat_copy(d).wait_recv()
        whole = stat_all[0]
        for g in range(1, users):
            whole = whole + stat_all[g]
        panel_mean = whole[0:1, :] / whole[8:9, :]
        for g in range(users):
            delta = stat_all[g, 0:1, :] / stat_all[g, 8:9, :] - panel_mean
            shift[g] = jnp.broadcast_to(delta, (width, P_SIZE)).T
        for d in range(1, users):
            sum_copy(d).wait_recv()
        means = sums_all[0]
        for g in range(1, users):
            means = means + sums_all[g]
        mean_mine[...] = means / whole[8:9, 0:1]
        for d in range(1, items):
            mean_copy(d).start()
        mean_all[item] = mean_mine[...]

    def finish(n):
        f, c = lax.div(n, cyc), lax.rem(n, cyc)
        home(n)

        @pl.when(z_first(n))
        def _():
            i = lax.div(n, EVERY)
            for d in range(1, xn):
                late_copy(n, d).wait_recv()
                code = late_recv[i, d - 1, COLS : COLS + EXTRA, :].astype(jnp.int32).astype(f32)[0:1]
                own[n, z] = own[n, z] + decode(late_recv[i, d - 1, 0:COLS, :], code)

        value = own[n, z]
        for g in range(users):
            part = pl.ds(pl.multiple_of(f * COLS, COLS), COLS)
            value = value + shift[g, part, :] * sums_all[g, pl.ds(c, 1), :]
        total = stat_all[0, 8:9, 0:1]
        for g in range(1, users):
            total = total + stat_all[g, 8:9, 0:1]
        icov[n] = (value / total).T
        for d in range(1, items):
            item_copy(n, d).start()
        part = pl.ds(pl.multiple_of(f * COLS, COLS), COLS)
        cov_ref[item * cyc + c, :, part] = icov[n, pl.ds(pl.multiple_of(item * BLK, BLK), BLK), :]

    lag = min(LAG, units)
    hops = zn - 1
    last = cyc + lag + hops

    def step(s, _):
        @pl.when(s < units)
        def _():
            compute(s)

        @pl.when(s == min(1, cyc - 1))
        def _():
            for f in range(1, PHASES):
                panel_back(f)

        @pl.when(s == min(3, cyc - 1))
        def _():
            for f in range(1, PHASES):
                panel_weigh(f)
            for d in range(1, users):
                stat_copy(d).start()

        @pl.when(s == cyc - 1)
        def _():
            for d in range(1, users):
                sum_copy(d).start()

        @pl.when(s >= lag)
        def _():
            @pl.when((s < units + lag) & jnp.logical_not(z_first(s - lag)))
            def _():
                relay(s - lag)

        for h in range(hops):
            @pl.when((s >= lag + h) & (s < units + lag + h))
            def _():
                hop(s - lag - h, h)

        @pl.when((s >= lag + hops) & (s < units + lag + hops) & z_first(s - lag - hops))
        def _():
            late(s - lag - hops)

        @pl.when(s == last)
        def _():
            statistics()

        @pl.when(s >= last)
        def _():
            for k in range(PHASES):
                finish((s - last) * PHASES + k)

        return 0

    lax.fori_loop(0, units + lag + hops, step, 0)

    for d in range(1, items):
        mean_copy(d).wait()
    for i in range(items):
        value = jnp.zeros((mean_all.shape[1], BLK), f32)
        for k in range(items):
            value = jnp.where(item == k, mean_all[i, :, k * BLK : (k + 1) * BLK], value)
        mean_ref[i * cyc : (i + 1) * cyc, :] = value[0:cyc]

    for f in range(PHASES):
        for p in range(PIECES):
            near_copy(f, p).wait_send()
            back_copy(f, p).wait_send()
            for d in range(1, yn):
                far_copy(f, p, d).wait_send()
    for d in range(1, users):
        stat_copy(d).wait_send()
        sum_copy(d).wait_send()

    def drain(n, _):
        @pl.when(z_first(n))
        def _():
            for d in range(1, xn):
                late_copy(n, d).wait_send()

        @pl.when(jnp.logical_not(z_first(n)))
        def _():
            for d in range(1, xn):
                x_copy(n, d).wait_send()

        for k in range(zn):
            @pl.when(z != k)
            def _():
                z_copy(n, k, k, lax.rem(z + 1, zn)).wait_send()

                @pl.when(z_first(n))
                def _():
                    for d in range(1, xn):
                        z_copy(beside(n, d), k, k, lax.rem(z + 1, zn)).wait_send()

        for d in range(1, items):
            item_copy(n, d).wait()
        return 0

    lax.fori_loop(0, units, drain, 0)


def hand_over_kernel(cov_ref, mean_ref, cov_out, mean_out, sem):
    whole = pltpu.make_async_copy(cov_ref, cov_out, sem.at[0])
    means = pltpu.make_async_copy(mean_ref, mean_out, sem.at[1])
    whole.start()
    means.start()
    whole.wait()
    means.wait()


def hand_over(cov, mean):
    anywhere = pl.BlockSpec(memory_space=pl.ANY)
    vmem = pl.BlockSpec(memory_space=pltpu.VMEM)
    return pl.pallas_call(
        hand_over_kernel,
        out_shape=(
            jax.ShapeDtypeStruct(cov.shape, f32), jax.ShapeDtypeStruct(mean.shape, f32),
        ),
        in_specs=[vmem, vmem],
        out_specs=(anywhere, anywhere),
        scratch_shapes=[pltpu.SemaphoreType.DMA((2,))],
        name="hand_over",
    )(cov, mean)


def per_device(interactions, user_weights, panel_index):
    rows, shard = interactions.shape
    users, items = lax.axis_size("users"), lax.axis_size("items")
    zn = 4 if users % 4 == 0 else 1
    xn = users // zn
    width = items * BLK
    cyc = shard // (users * width)
    cyc8 = -(-cyc // 8) * 8
    yn = items // 2
    per_shard = shard // P_SIZE
    chosen = panel_index[0]
    local = lax.dynamic_slice_in_dim(interactions, chosen % per_shard * P_SIZE, P_SIZE, 1)
    local = jnp.where(lax.axis_index("items") == chosen // per_shard, local, jnp.zeros_like(local))
    weights = user_weights.reshape(rows // 128, 128)

    bf16, i16 = jnp.bfloat16, jnp.int16
    piece, tall = COLS // 2 // PIECES, COLS + EXTRA
    pieces, units = PHASES * PIECES, PHASES * cyc
    firsts = (units + EVERY - 1 - FIRST) // EVERY
    chains, firsts = units + firsts * (xn - 1), max(firsts, 1)
    dma = pltpu.SemaphoreType.DMA
    vmem = pl.BlockSpec(memory_space=pltpu.VMEM)
    cov, mean = pl.pallas_call(
        functools.partial(kernel, (users, items, xn, zn, cyc, width)),
        out_shape=(
            jax.ShapeDtypeStruct((items * cyc, BLK, P_SIZE), f32),
            jax.ShapeDtypeStruct((items * cyc, BLK), f32),
        ),
        in_specs=[pl.BlockSpec(memory_space=pl.ANY), vmem, vmem],
        out_specs=(vmem, vmem),
        scratch_shapes=[
            pltpu.VMEM((cyc, rows, users * width), bf16),
            pltpu.VMEM((P_SIZE, rows), bf16),
            pltpu.VMEM((P_SIZE, rows), bf16),
            pltpu.VMEM((pieces, piece, rows), bf16),
            pltpu.VMEM((pieces, piece, rows), bf16),
            pltpu.VMEM((pieces, yn - 1, piece, rows), bf16),
            pltpu.VMEM((PHASES, tall, rows), bf16),
            pltpu.VMEM((P_SIZE, 128), f32),
            pltpu.VMEM((COLS, users * width), f32),
            pltpu.VMEM((chains, zn, COLS, width), f32),
            pltpu.VMEM((units, xn - 1, zn * COLS + EXTRA, width), i16),
            pltpu.VMEM((units, xn - 1, zn * COLS + EXTRA, width), i16),
            pltpu.VMEM((firsts, xn - 1, tall, width), i16),
            pltpu.VMEM((firsts, xn - 1, tall, width), i16),
            pltpu.VMEM((chains, zn, tall, width), i16),
            pltpu.VMEM((chains, zn + 1, tall, width), i16),
            pltpu.VMEM((units, width, COLS), f32),
            pltpu.VMEM((users, cyc8, width), f32),
            pltpu.VMEM((users, cyc8, width), f32),
            pltpu.VMEM((16, P_SIZE), f32),
            pltpu.VMEM((users, 16, P_SIZE), f32),
            pltpu.VMEM((users, P_SIZE, width), f32),
            pltpu.VMEM((cyc8, width), f32),
            pltpu.VMEM((items, cyc8, width), f32),
            dma((cyc,)),
            dma((pieces,)), dma((pieces,)),
            dma((pieces, yn - 1)), dma((pieces, yn - 1)),
            dma((pieces,)), dma((pieces,)),
            dma((units, xn - 1)), dma((units, xn - 1)),
            dma((firsts, xn - 1)), dma((firsts, xn - 1)),
            dma((chains, zn)), dma((chains, zn + 1)),
            dma((units, items - 1)), dma((units, items - 1)),
            dma((users - 1,)), dma((users - 1,)),
            dma((users - 1,)), dma((users - 1,)),
            dma((items - 1,)), dma((items - 1,)),
        ],
        compiler_params=pltpu.CompilerParams(
            collective_id=0, has_side_effects=True, vmem_limit_bytes=61 * 2**20
        ),
        cost_estimate=pl.CostEstimate(
            flops=2 * P_SIZE * rows * shard, bytes_accessed=2 * rows * shard, transcendentals=0
        ),
        name="panel_covariance",
    )(interactions, local, weights)
    return hand_over(cov, mean)


def solution(mesh):
    return jax.shard_map(
        per_device,
        mesh=mesh,
        in_specs=(P("users", "items"), P("users"), P()),
        out_specs=(P(None, ("users", "items"), None), P(None, ("users", "items"))),
        check_vma=False,
    )
```
